128 devices in a mesh: ab: 32 (over z, x, core), cd: 4 (over y).
Axes of the slice: x: 4, y: 4, z: 4, core: 2. Of those that a mesh axis runs over, the one named last changes fastest.
Arguments:
- amplitudes: bfloat16 [2048, 16384], P('ab', 'cd'), may hold values from -6 to 6
- integrals: bfloat16 [16384, 40960], P('cd', 'ab'), may hold values from -0.125 to 0.125
- ab_sizes: int32 [8], replicated, may hold values from 128 to 20480, as said below
- cd_sizes: int32 [8], replicated, may hold values from 512 to 8192, as said below
- virt_energy: float32 [40960], P('ab'), may hold values from 1 to 4
- occ_energy: float32 [2048], P('cd'), may hold values from -2 to -0.5
Outputs:
- residual: float32 [2048, 40960], P('cd', 'ab')
- update: float32 [2048, 40960], P('cd', 'ab')
The draws below stay inside these ranges and needn't reach their ends.
Inputs may be any that keep to these rules, and one draw needn't show every extreme that they name: `ab_sizes`: each entry is a positive multiple of 128; the 8 entries sum to 40960. `cd_sizes`: each entry is a positive multiple of 512; the 8 entries sum to 16384.
All inputs are finite; a program needn't handle non-finite values.
Results may differ from the reference program's by a relative error of at most 0.0003.
Values may be sent and summed in bfloat16 or wider, within the bound.
A program may use at most 256 MiB of HBM per device.

```python
import jax
import jax.numpy as jnp
from jax import lax

OCC = 2048
NIRR = 8
AB = 40960
CD = 16384
TAB = 128
TCD = 512


def spread_sizes(key, tiles, tile_size):
    first, second, third = jax.random.split(key, 3)
    order = jax.random.permutation(first, NIRR)
    largest = order[0]
    smallest = order[1]
    labels = jnp.arange(NIRR, dtype=jnp.int32)
    others = jnp.logical_and(labels != largest, labels != smallest)
    weights = jnp.where(others, jax.random.randint(second, (NIRR,), 1, 5), 0)
    bounds = jnp.cumsum(weights)
    most = tiles // 2
    extra = tiles - most - 1 - (NIRR - 2)
    picks = jax.random.randint(third, (extra,), 0, bounds[-1])
    owner = jnp.sum((picks[:, None] >= bounds[None, :]).astype(jnp.int32), axis=1)
    counts = 1 + jnp.sum((owner[:, None] == labels[None, :]).astype(jnp.int32), axis=0)
    counts = jnp.where(labels == largest, most, jnp.where(labels == smallest, 1, counts))
    return (counts * tile_size).astype(jnp.int32)


def draw_ab_sizes(key, part):
    key = jax.random.fold_in(key, 11)
    return spread_sizes(key, AB // TAB, TAB)


def draw_cd_sizes(key, part):
    key = jax.random.fold_in(key, 23)
    return spread_sizes(key, CD // TCD, TCD)


def shard_levels(key, extent, shards, low, high):
    def one(position, blocks):
        heights = jax.random.uniform(jax.random.fold_in(jax.random.fold_in(key, 6), position), (blocks,), jnp.float32, low / len(shards), high / len(shards))
        return jnp.repeat(jnp.exp(heights), extent[position] // blocks).reshape((-1,) + (1,) * (len(extent) - position - 1))

    loudness = one(*shards[0])
    for cut in shards[1:]:
        loudness = loudness * one(*cut)
    return loudness


def noise(key, shape, spread, most, pieces=(), kind=jnp.bfloat16):
    values = spread * jax.random.normal(key, shape, jnp.float32)
    if pieces:
        values = values * shard_levels(key, shape, pieces, -0.22, 0.18)
    return jnp.clip(values, -most, most).astype(kind)


def setup_inputs(seed: int = 0) -> dict:
    keys = jax.random.split(jax.random.key(seed), 7)
    return {
        "amplitudes": noise(keys[0], (OCC, CD), 1.0, 6.0, ((0, 32), (1, 4))),
        "integrals": noise(keys[1], (CD, AB), (CD // NIRR) ** -0.5, 0.125, ((0, 4), (1, 32))),
        "ab_sizes": draw_ab_sizes(jax.random.fold_in(keys[6], 71), 0),
        "cd_sizes": draw_cd_sizes(jax.random.fold_in(keys[6], 71), 0),
        "virt_energy": jnp.clip(1.0 + 3.0 * jax.random.uniform(keys[4], (AB,), jnp.float32) ** shard_levels(keys[4], (AB,), ((0, 32),), -0.2, 0.2), 1.0, 4.0),
        "occ_energy": jnp.clip(-2.0 + 1.5 * jax.random.uniform(keys[5], (OCC,), jnp.float32) ** shard_levels(keys[5], (OCC,), ((0, 4),), -0.2, 0.2), -2.0, -0.5),
    }


def irrep_of(sizes, positions):
    ends = jnp.cumsum(sizes).astype(jnp.int32)
    return jnp.sum((positions[:, None] >= ends[None, :]).astype(jnp.int32), axis=1).astype(jnp.int32)


def reference(amplitudes, integrals, ab_sizes, cd_sizes, virt_energy, occ_energy):
    ab_irrep = irrep_of(ab_sizes, jnp.arange(AB, dtype=jnp.int32))
    tile_count = CD // TCD
    tile_irrep = irrep_of(cd_sizes, jnp.arange(tile_count, dtype=jnp.int32) * TCD)

    def add_tile(total, index):
        start = (index * TCD).astype(jnp.int32)
        left = lax.dynamic_slice_in_dim(amplitudes, start, TCD, 1)
        right = lax.dynamic_slice_in_dim(integrals, start, TCD, 0)
        product = jnp.dot(left, right, preferred_element_type=jnp.float32)
        chosen = jnp.sum(jnp.where(jnp.arange(tile_count, dtype=jnp.int32) == index, tile_irrep, 0))
        return total + jnp.where(ab_irrep[None, :] == chosen, product, jnp.float32(0.0)), None

    start_total = jnp.zeros((OCC, AB), jnp.float32)
    residual, _ = lax.scan(add_tile, start_total, jnp.arange(tile_count, dtype=jnp.int32))
    update = residual / (virt_energy[None, :] - occ_energy[:, None])
    return residual, update
```

```python
import functools

import jax
import jax.numpy as jnp
from jax import lax
from jax.experimental import pallas as pl
from jax.experimental.pallas import tpu as pltpu
from jax.sharding import PartitionSpec as P

MESH = pl.DeviceIdType.MESH
TCD = 512
LANES = 128
TOP = 32000.0
FINE = 64.0

ORDER = (
    (0, 0), (1, 0), (3, 0), (0, 1), (0, 3), (2, 0), (0, 2), (1, 1),
    (1, 3), (1, 2), (3, 1), (3, 3), (3, 2), (2, 1), (2, 3), (2, 2),
)
SLOT = {d: k for k, d in enumerate(ORDER)}
STEPS = len(ORDER)
HANDLE = {1: (1, 2), 2: (3, 4), 4: (5, 6), 6: (7, 8), 8: (9,), 9: (10, 11), 11: (12,), 12: (13, 14), 14: (15,)}
NEAR_LAG = 1
OWN_LAG = 2


def pick(table, index):
    value = 0
    for k, v in enumerate(table):
        if v:
            value = value + jnp.where(index == k, v, 0)
    return value


def forwards(k):
    dp, dq = ORDER[k]
    out = []
    if dq == 0:
        if dp == 0:
            out.append((None, "p+", SLOT[3, 0]))
            out.append((None, "p-", SLOT[1, 0]))
        elif dp == 3:
            out.append((0, "p+", SLOT[2, 0]))
        elif dp == 1:
            out.append((1, "p-", SLOT[2, 0]))
        out.append((None, "q+", SLOT[dp, 3]))
        out.append((None, "q-", SLOT[dp, 1]))
    elif dq == 3:
        out.append((0, "q+", SLOT[dp, 2]))
    elif dq == 1:
        out.append((1, "q-", SLOT[dp, 2]))
    return out


SENDS = [(k, *copy) for k in range(STEPS) for copy in forwards(k)]


def in_halves(k):
    return 2 in ORDER[k] and ORDER[k] != (2, 1) and ORDER[k] != (2, 3)


def kernel(
    ab_sizes, cd_sizes, amp, integ, out,
    gath, right, acc, nearbuf, resbuf, far_s, far_r, near_s, near_r,
    amp_sem, int_sem, out_sem, ag_s, ag_r, sib_s, sib_r, far_ss, far_rs, near_ss, near_rs,
):
    cd_local, ab_local = right.shape
    unit = amp.shape[0]
    half = unit // 2
    blocks = ab_local // LANES
    index = lax.axis_index("ab")
    y = lax.axis_index("cd")
    c = index % 2
    x = (index // 2) % 4
    z = index // 8

    def at(z_, x_, c_):
        return ((z_ % 4) * 4 + x_ % 4) * 2 + c_

    def along(step, second):
        over_x = (1 - c) * (1 - second) + c * second
        return (at(z + step * (1 - over_x), x + step * over_x, c), y)

    target = {
        "p+": along(1, 0), "p-": along(3, 0), "q+": along(1, 1), "q-": along(3, 1),
        "core": (at(z, x, 1 - c), y), "y+": (index, (y + 1) % 4), "y-": (index, (y + 3) % 4),
    }

    tile_count = cd_local // TCD

    def int_copy(t):
        rows = pl.ds(pl.multiple_of(t * TCD, TCD), TCD)
        return pltpu.make_async_copy(integ.at[rows], right.at[rows], int_sem.at[t])

    amp_copy = pltpu.make_async_copy(amp, gath.at[0, 0], amp_sem)
    amp_copy.start()
    for t in range(tile_count):
        int_copy(t).start()

    barrier = pltpu.get_barrier_semaphore()
    for name in target:
        pl.semaphore_signal(barrier, inc=1, device_id=target[name], device_id_type=MESH)
    pl.semaphore_wait(barrier, len(target))

    def gather_copy(number, k, part, direction, slot):
        source = amp if k == 0 else gath.at[k, 0]
        dest = gath.at[slot, 0]
        if part is not None:
            source = source.at[pl.ds(part * half, half)]
            dest = dest.at[pl.ds(part * half, half)]
        return pltpu.make_async_remote_copy(
            src_ref=source, dst_ref=dest, send_sem=ag_s.at[number], recv_sem=ag_r.at[slot, part or 0],
            device_id=target[direction], device_id_type=MESH,
        )

    def sibling_copy(k):
        return pltpu.make_async_remote_copy(
            src_ref=amp if k == 0 else gath.at[k, 0], dst_ref=gath.at[k, 1],
            send_sem=sib_s.at[k], recv_sem=sib_r.at[k],
            device_id=target["core"], device_id_type=MESH,
        )

    def handle(k):
        if k:
            for part in (0, 1) if in_halves(k) else (None,):
                dest = gath.at[k, 0]
                if part is not None:
                    dest = dest.at[pl.ds(part * half, half)]
                pltpu.make_async_remote_copy(
                    src_ref=dest, dst_ref=dest, send_sem=ag_s.at[0], recv_sem=ag_r.at[k, part or 0],
                    device_id=target["p+"], device_id_type=MESH,
                ).wait_recv()
        for number, copy in enumerate(SENDS):
            if copy[0] == k:
                gather_copy(number, *copy).start()
        sibling_copy(k).start()

    handle(0)

    column = index * ab_local + lax.broadcasted_iota(jnp.int32, (1, ab_local), 1)

    def mask_tile(t, carry):
        place = y * cd_local + t * TCD
        low = 0
        high = 0
        end = 0
        for h in range(8):
            size = ab_sizes[h]
            high = high + jnp.where(end <= place, size, 0)
            end = end + cd_sizes[h]
            low = low + jnp.where(end <= place, size, 0)
        keep = jnp.where(jnp.logical_and(column >= low, column < high), 1.0, 0.0).astype(jnp.bfloat16)
        int_copy(t).wait()
        rows = pl.ds(pl.multiple_of(t * TCD, TCD), TCD)
        right[rows, :] = right[rows, :] * keep
        return carry

    lax.fori_loop(0, tile_count, mask_tile, 0)
    amp_copy.wait()

    def unit_place(s, net):
        dp = pick([d[0] for d in ORDER], s)
        dq = pick([d[1] for d in ORDER], s)
        core = (c + net) % 2
        dz = dq + core * (dp - dq)
        dx = dp + core * (dq - dp)
        return (z + dz - y + 8) % 4, ((x + dx) % 4) * 2 + core

    row_of = lax.broadcasted_iota(jnp.int32, (16, LANES), 0)

    def quantize(source, row, rows, dest):
        scales = jnp.zeros((16, LANES), jnp.float32)
        for j in range(blocks):
            value = source[pl.ds(row, rows), pl.ds(j * LANES, LANES)]
            most = jnp.max(jnp.abs(value), axis=0, keepdims=True)
            code = jnp.ceil(jnp.log2(jnp.maximum(most, 1e-30)) * FINE)
            factor = TOP / jnp.exp2(code * (1.0 / FINE))
            whole = jnp.floor(value * factor + 0.5).astype(jnp.int32).astype(jnp.int16)
            for i in range(rows // 16):
                dest[j * (rows // 16) + i] = whole[i * 16 : (i + 1) * 16]
            scales = jnp.where(row_of == j, code, scales)
        dest[blocks * (rows // 16)] = scales.astype(jnp.int32).astype(jnp.int16)

    def scales_of(source, rows):
        code = source[blocks * (rows // 16)].astype(jnp.int32).astype(jnp.float32)
        return jnp.exp2(code * (1.0 / FINE)) * (1.0 / TOP)

    def tiles_of(source, rows, j, scales):
        parts = [source[j * (rows // 16) + i].astype(jnp.int32).astype(jnp.float32) for i in range(rows // 16)]
        return jnp.concatenate(parts, axis=0) * scales[j : j + 1]

    def far_copy(slot, side):
        return pltpu.make_async_remote_copy(
            src_ref=far_s.at[side, slot], dst_ref=far_r.at[side, slot],
            send_sem=far_ss.at[side, slot], recv_sem=far_rs.at[side, slot],
            device_id=target["y-" if side else "y+"], device_id_type=MESH,
        )

    def near_copy(slot, side):
        return pltpu.make_async_remote_copy(
            src_ref=near_s.at[side, slot], dst_ref=near_r.at[side, slot],
            send_sem=near_ss.at[side, slot], recv_sem=near_rs.at[side, slot],
            device_id=target["y-" if side else "y+"], device_id_type=MESH,
        )

    def out_copy(slot):
        rows = pl.ds(pl.multiple_of(slot * unit, unit), unit)
        return pltpu.make_async_copy(resbuf.at[slot], out.at[rows], out_sem.at[slot])

    def after_product(s, net):
        role, slot = unit_place(s, net)

        @pl.when(role == 2)
        def _():
            for side in (0, 1):
                quantize(acc, net * unit + side * half, half, far_s.at[side, slot])
                far_copy(slot, side).start()

        for side, near in ((0, 1), (1, 3)):

            @pl.when(role == near)
            def _():
                nearbuf[side, slot] = acc[pl.ds(net * unit, unit), :]

        @pl.when(role == 0)
        def _():
            resbuf[slot] = acc[pl.ds(net * unit, unit), :]

    def near_stage(s, net):
        role, slot = unit_place(s, net)
        for side, near in ((0, 1), (1, 3)):

            @pl.when(role == near)
            def _():
                far_copy(slot, side).wait_recv()
                arrived = far_r.at[side, slot]
                scales = scales_of(arrived, half)
                for j in range(blocks):
                    cols = pl.ds(j * LANES, LANES)
                    rows = pl.ds(side * half, half)
                    nearbuf[side, slot, rows, cols] = nearbuf[side, slot, rows, cols] + tiles_of(arrived, half, j, scales)
                quantize(nearbuf.at[side, slot], 0, unit, near_s.at[side, slot])
                near_copy(slot, side).start()

    def own_stage(s, net):
        role, slot = unit_place(s, net)

        @pl.when(role == 0)
        def _():
            for side in (0, 1):
                near_copy(slot, side).wait_recv()
                arrived = near_r.at[side, slot]
                scales = scales_of(arrived, unit)
                for j in range(blocks):
                    cols = pl.ds(j * LANES, LANES)
                    resbuf[slot, :, cols] = resbuf[slot, :, cols] + tiles_of(arrived, unit, j, scales)
            out_copy(slot).start()

    def step(s, carry):
        for k, slots in HANDLE.items():

            @pl.when(s == k)
            def _():
                for slot in slots:
                    handle(slot)

        @pl.when(s < STEPS)
        def _():
            pltpu.make_async_remote_copy(
                src_ref=gath.at[s, 1], dst_ref=gath.at[s, 1], send_sem=sib_s.at[s], recv_sem=sib_r.at[s],
                device_id=target["core"], device_id_type=MESH,
            ).wait_recv()
            left = gath[s].reshape(2 * unit, cd_local)
            acc[...] = jnp.dot(left, right[...], preferred_element_type=jnp.float32)
            for net in (0, 1):
                after_product(s, net)

        @pl.when(jnp.logical_and(s >= NEAR_LAG, s < STEPS + NEAR_LAG))
        def _():
            for net in (0, 1):
                near_stage(s - NEAR_LAG, net)

        @pl.when(s >= OWN_LAG)
        def _():
            for net in (0, 1):
                own_stage(s - OWN_LAG, net)

        return carry

    lax.fori_loop(0, STEPS + OWN_LAG, step, 0)

    for number, copy in enumerate(SENDS):
        gather_copy(number, *copy).wait_send()
    for k in range(STEPS):
        sibling_copy(k).wait_send()

    def finish(slot, carry):
        for side in (0, 1):
            far_copy(slot, side).wait_send()
            near_copy(slot, side).wait_send()
        out_copy(slot).wait()
        return carry

    lax.fori_loop(0, 8, finish, 0)


def body(amplitudes, integrals, ab_sizes, cd_sizes, virt_energy, occ_energy):
    cd_local, ab_local = integrals.shape
    unit = amplitudes.shape[0]
    rows = occ_energy.shape[0]
    blocks = ab_local // LANES
    far = blocks * (unit // 32) + 1
    near = blocks * (unit // 16) + 1
    dma = pltpu.SemaphoreType.DMA
    residual = pl.pallas_call(
        kernel,
        out_shape=jax.ShapeDtypeStruct((rows, ab_local), jnp.float32),
        in_specs=[pl.BlockSpec(memory_space=pltpu.SMEM)] * 2 + [pl.BlockSpec(memory_space=pl.ANY)] * 2,
        out_specs=pl.BlockSpec(memory_space=pl.ANY),
        scratch_shapes=[
            pltpu.VMEM((STEPS, 2, unit, cd_local), jnp.bfloat16),
            pltpu.VMEM((cd_local, ab_local), jnp.bfloat16),
            pltpu.VMEM((2 * unit, ab_local), jnp.float32),
            pltpu.VMEM((2, 8, unit, ab_local), jnp.float32),
            pltpu.VMEM((8, unit, ab_local), jnp.float32),
            pltpu.VMEM((2, 8, far, 16, LANES), jnp.int16),
            pltpu.VMEM((2, 8, far, 16, LANES), jnp.int16),
            pltpu.VMEM((2, 8, near, 16, LANES), jnp.int16),
            pltpu.VMEM((2, 8, near, 16, LANES), jnp.int16),
            dma, dma((cd_local // TCD,)), dma((8,)), dma((20,)), dma((STEPS, 2)), dma((STEPS,)), dma((STEPS,)),
            dma((2, 8)), dma((2, 8)), dma((2, 8)), dma((2, 8)),
        ],
        compiler_params=pltpu.CompilerParams(
            collective_id=0, has_side_effects=True, vmem_limit_bytes=60 * 2**20
        ),
    )(ab_sizes, cd_sizes, amplitudes, integrals)
    update = residual / (virt_energy[None, :] - occ_energy[:, None])
    return (residual, update)


def solution(mesh):
    placed = (P("ab", "cd"), P("cd", "ab"), P(), P(), P("ab"), P("cd"))
    return jax.shard_map(
        body, mesh=mesh, in_specs=placed, out_specs=(P("cd", "ab"), P("cd", "ab")), check_vma=False
    )
```

```python
import functools

import jax
import jax.numpy as jnp
from jax import lax
from jax.experimental import pallas as pl
from jax.experimental.pallas import tpu as pltpu
from jax.sharding import PartitionSpec as P

MESH = pl.DeviceIdType.MESH
TCD = 512
LANES = 128
TOP = 32000.0
FINE = 64.0

GROUPS = ((4, 12), (8,)) + tuple((4 * d + 1, 4 * d + 3) for d in range(4)) + tuple((4 * d + 2,) for d in range(4))
PASSED = ((0,), (4, 12), (8,))
STEPS = 16

ACTIONS = (
    (
        5, 20, 4096, 3, 3104, 1, 129, 13, 28, 12, 44, 7328, 33, 19, 5000, 97, 2, 776,
        21, 36, 52, 130, 161, 27, 60, 225, 5568, 137, 153, 11, 2232, 34, 162, 226, 1832, 193,
        9, 25, 98, 65, 43, 7440, 169, 1784, 138, 35, 7112, 68, 76, 17, 10, 26, 185, 194,
        51, 154, 170, 57, 49, 2448, 59, 201, 41, 233, 217, 5720, 67, 249, 58, 66, 18, 145,
        3536, 75, 7800, 186, 50, 234, 202, 73, 250, 218, 42, 89, 177, 3664, 209, 146, 121, 105,
        241, 74, 210, 90, 178, 81, 113, 122, 242, 82, 106, 114,
    ),
    (
        5, 20, 4096, 3, 12, 3104, 1, 13, 28, 7328, 129, 33, 19, 52, 97, 5000, 11, 2056,
        161, 225, 2, 34, 130, 98, 65, 27, 60, 6056, 9, 137, 153, 51, 4648, 21, 36, 44,
        1816, 59, 5824, 138, 145, 66, 162, 154, 226, 3944, 25, 185, 169, 177, 193, 35, 68, 7112,
        2888, 41, 146, 10, 186, 178, 57, 43, 76, 7952, 105, 121, 1768, 67, 73, 89, 6736, 75,
        201, 217, 3824, 17, 249, 170, 26, 194, 42, 58, 106, 233, 122, 49, 81, 209, 74, 202,
        218, 18, 90, 113, 241, 82, 210, 250, 234, 242, 50, 114,
    ),
)


def pick(table, index):
    words = [low + 8192 * high for low, high in zip(table[::2], table[1::2] + (0,))]
    at = index // 2
    word = words[0]
    for w in range(1, len(words)):
        word = jnp.where(at == w, words[w], word)
    return jnp.where(index % 2 == 0, word, word // 8192) % 8192


def kernel(
    ab_sizes, cd_sizes, amp, integ, out,
    gath, right, acc, nearbuf, resbuf, far_s, far_r, near_s, near_r,
    amp_sem, int_sem, out_sem, ag_s, ag_r, sib_s, sib_r, far_ss, far_rs, near_ss, near_rs,
):
    cd_local, ab_local = right.shape
    unit = amp.shape[0]
    half = unit // 2
    blocks = ab_local // LANES
    index = lax.axis_index("ab")
    y = lax.axis_index("cd")
    c = index % 2
    x = (index // 2) % 4
    z = index // 8

    def at(z_, x_, c_):
        return ((z_ % 4) * 4 + x_ % 4) * 2 + c_

    def along(step):
        return (at(z + step * c, x + step * (1 - c), c), y)

    target = {
        "+": along(1), "-": along(3),
        "core": (at(z, x, 1 - c), y), "y+": (index, (y + 1) % 4), "y-": (index, (y + 3) % 4),
    }

    tile_count = cd_local // TCD

    def int_copy(t):
        rows = pl.ds(pl.multiple_of(t * TCD, TCD), TCD)
        return pltpu.make_async_copy(integ.at[rows], right.at[rows], int_sem.at[t])

    amp_copy = pltpu.make_async_copy(amp, gath.at[0, 0], amp_sem)
    amp_copy.start()
    for t in range(tile_count):
        int_copy(t).start()

    barrier = pltpu.get_barrier_semaphore()
    for name in target:
        pl.semaphore_signal(barrier, inc=1, device_id=target[name], device_id_type=MESH)
    pl.semaphore_wait(barrier, len(target))

    def gather_copy(g, side):
        part = None
        if g == 0:
            source, slot, gather = amp, (12, 4)[side], 0
        elif g == 1:
            source, slot, gather, part = gath.at[(12, 4)[side], 0], 8, 0, side
        elif g < 6:
            d = 4 * (g - 2)
            source, slot, gather = gath.at[d, 1], d + (3, 1)[side], 1
        else:
            d = 4 * (g - 6)
            source, slot, gather, part = gath.at[d + (3, 1)[side], 1], d + 2, 1, side
        dest = gath.at[slot, gather]
        if part is not None:
            source = source.at[pl.ds(part * half, half)]
            dest = dest.at[pl.ds(part * half, half)]
        return pltpu.make_async_remote_copy(
            src_ref=source, dst_ref=dest, send_sem=ag_s.at[g, side], recv_sem=ag_r.at[slot, part or 0],
            device_id=target["-" if side else "+"], device_id_type=MESH,
        )

    def sibling_copy(k):
        gather = 0 if k % 4 == 0 else 1
        return pltpu.make_async_remote_copy(
            src_ref=amp if k == 0 else gath.at[k, gather], dst_ref=gath.at[k, 1 - gather],
            send_sem=sib_s.at[k], recv_sem=sib_r.at[k],
            device_id=target["core"], device_id_type=MESH,
        )

    def issue(g):
        for side in (0, 1):
            gather_copy(g, side).start()

    def handle(g):
        for side in (0, 1):
            gather_copy(g, side).wait_recv()
        for k in GROUPS[g]:
            sibling_copy(k).start()

    def passed(g):
        for k in PASSED[g]:
            pltpu.make_async_remote_copy(
                src_ref=gath.at[k, 1], dst_ref=gath.at[k, 1], send_sem=sib_s.at[k], recv_sem=sib_r.at[k],
                device_id=target["core"], device_id_type=MESH,
            ).wait_recv()

    issue(0)
    sibling_copy(0).start()

    column = index * ab_local + lax.broadcasted_iota(jnp.int32, (1, ab_local), 1)

    def mask_tile(t, carry):
        place = y * cd_local + t * TCD
        low = 0
        high = 0
        end = 0
        for h in range(8):
            size = ab_sizes[h]
            high = high + jnp.where(end <= place, size, 0)
            end = end + cd_sizes[h]
            low = low + jnp.where(end <= place, size, 0)
        keep = jnp.where(jnp.logical_and(column >= low, column < high), 1.0, 0.0).astype(jnp.bfloat16)
        int_copy(t).wait()
        rows = pl.ds(pl.multiple_of(t * TCD, TCD), TCD)
        right[rows, :] = right[rows, :] * keep
        return carry

    lax.fori_loop(0, tile_count, mask_tile, 0)
    amp_copy.wait()

    def unit_place(u):
        net = u // 16
        dp = (u % 16) // 4
        dq = u % 4
        core = (c + net) % 2
        dz = dq + core * (dp - dq)
        dx = dp + core * (dq - dp)
        return (z + dz - y + 8) % 4, ((x + dx) % 4) * 2 + core

    row_of = lax.broadcasted_iota(jnp.int32, (16, LANES), 0)

    def quantize(source, row, rows, dest):
        scales = jnp.zeros((16, LANES), jnp.float32)
        for j in range(blocks):
            value = source[pl.ds(row, rows), pl.ds(j * LANES, LANES)]
            most = jnp.max(jnp.abs(value), axis=0, keepdims=True)
            code = jnp.ceil(jnp.log2(jnp.maximum(most, 1e-30)) * FINE)
            factor = TOP / jnp.exp2(code * (1.0 / FINE))
            whole = jnp.floor(value * factor + 0.5).astype(jnp.int32).astype(jnp.int16)
            for i in range(rows // 16):
                dest[j * (rows // 16) + i] = whole[i * 16 : (i + 1) * 16]
            scales = jnp.where(row_of == j, code, scales)
        dest[blocks * (rows // 16)] = scales.astype(jnp.int32).astype(jnp.int16)

    def scales_of(source, rows):
        code = source[blocks * (rows // 16)].astype(jnp.int32).astype(jnp.float32)
        return jnp.exp2(code * (1.0 / FINE)) * (1.0 / TOP)

    def tiles_of(source, rows, j, scales):
        parts = [source[j * (rows // 16) + i].astype(jnp.int32).astype(jnp.float32) for i in range(rows // 16)]
        return jnp.concatenate(parts, axis=0) * scales[j : j + 1]

    def far_copy(slot, side):
        return pltpu.make_async_remote_copy(
            src_ref=far_s.at[side, slot], dst_ref=far_r.at[side, slot],
            send_sem=far_ss.at[side, slot], recv_sem=far_rs.at[side, slot],
            device_id=target["y-" if side else "y+"], device_id_type=MESH,
        )

    def near_copy(slot, side):
        return pltpu.make_async_remote_copy(
            src_ref=near_s.at[side, slot], dst_ref=near_r.at[side, slot],
            send_sem=near_ss.at[side, slot], recv_sem=near_rs.at[side, slot],
            device_id=target["y-" if side else "y+"], device_id_type=MESH,
        )

    def out_copy(slot):
        rows = pl.ds(pl.multiple_of(slot * unit, unit), unit)
        return pltpu.make_async_copy(resbuf.at[slot], out.at[rows], out_sem.at[slot])

    def after_product(u, net):
        role, slot = unit_place(u)

        @pl.when(role == 2)
        def _():
            for side in (0, 1):
                quantize(acc, net * unit + side * half, half, far_s.at[side, slot])
                far_copy(slot, side).start()

        for side, near in ((0, 1), (1, 3)):

            @pl.when(role == near)
            def _():
                nearbuf[side, slot] = acc[pl.ds(net * unit, unit), :]

        @pl.when(role == 0)
        def _():
            resbuf[slot] = acc[pl.ds(net * unit, unit), :]

    def near_stage(u):
        role, slot = unit_place(u)
        for side, near in ((0, 1), (1, 3)):

            @pl.when(role == near)
            def _():
                far_copy(slot, side).wait_recv()
                arrived = far_r.at[side, slot]
                scales = scales_of(arrived, half)
                for j in range(blocks):
                    cols = pl.ds(j * LANES, LANES)
                    rows = pl.ds(side * half, half)
                    nearbuf[side, slot, rows, cols] = nearbuf[side, slot, rows, cols] + tiles_of(arrived, half, j, scales)
                quantize(nearbuf.at[side, slot], 0, unit, near_s.at[side, slot])
                near_copy(slot, side).start()

    def own_stage(u):
        role, slot = unit_place(u)

        @pl.when(role == 0)
        def _():
            for side in (0, 1):
                near_copy(slot, side).wait_recv()
                arrived = near_r.at[side, slot]
                scales = scales_of(arrived, unit)
                for j in range(blocks):
                    cols = pl.ds(j * LANES, LANES)
                    resbuf[slot, :, cols] = resbuf[slot, :, cols] + tiles_of(arrived, unit, j, scales)
            out_copy(slot).start()

    def product(first, second):
        for u in (first, second):

            @pl.when(jnp.logical_and(u < 16, u % 4 != 0))
            def _():
                pltpu.make_async_remote_copy(
                    src_ref=gath.at[u, 0], dst_ref=gath.at[u, 0], send_sem=sib_s.at[u], recv_sem=sib_r.at[u],
                    device_id=target["core"], device_id_type=MESH,
                ).wait_recv()

        left = jnp.concatenate([gath[u % 16, u // 16] for u in (first, second)], axis=0)
        acc[...] = jnp.dot(left, right[...], preferred_element_type=jnp.float32)
        after_product(first, 0)
        after_product(second, 1)

    def act(a, carry):
        code = jnp.where(c == 0, pick(ACTIONS[0], a), pick(ACTIONS[1], a))
        kind = code % 8
        arg = (code // 8) % 32

        @pl.when(kind == 0)
        def _():
            product(arg, code // 256)

        @pl.when(kind == 1)
        def _():
            near_stage(arg)

        @pl.when(kind == 2)
        def _():
            own_stage(arg)

        for this, count, do in ((3, len(GROUPS), handle), (4, len(GROUPS), issue), (5, len(PASSED), passed)):

            @pl.when(kind == this)
            def _():
                for g in range(count):

                    @pl.when(arg == g)
                    def _():
                        do(g)

        return carry

    lax.fori_loop(0, len(ACTIONS[0]), act, 0)

    for g in range(len(GROUPS)):
        for side in (0, 1):
            gather_copy(g, side).wait_send()
    for k in range(STEPS):
        sibling_copy(k).wait_send()

    def finish(slot, carry):
        for side in (0, 1):
            far_copy(slot, side).wait_send()
            near_copy(slot, side).wait_send()
        out_copy(slot).wait()
        return carry

    lax.fori_loop(0, 8, finish, 0)


def body(amplitudes, integrals, ab_sizes, cd_sizes, virt_energy, occ_energy):
    cd_local, ab_local = integrals.shape
    unit = amplitudes.shape[0]
    rows = occ_energy.shape[0]
    blocks = ab_local // LANES
    far = blocks * (unit // 32) + 1
    near = blocks * (unit // 16) + 1
    dma = pltpu.SemaphoreType.DMA
    residual = pl.pallas_call(
        kernel,
        out_shape=jax.ShapeDtypeStruct((rows, ab_local), jnp.float32),
        in_specs=[pl.BlockSpec(memory_space=pltpu.SMEM)] * 2 + [pl.BlockSpec(memory_space=pl.ANY)] * 2,
        out_specs=pl.BlockSpec(memory_space=pl.ANY),
        scratch_shapes=[
            pltpu.VMEM((STEPS, 2, unit, cd_local), jnp.bfloat16),
            pltpu.VMEM((cd_local, ab_local), jnp.bfloat16),
            pltpu.VMEM((2 * unit, ab_local), jnp.float32),
            pltpu.VMEM((2, 8, unit, ab_local), jnp.float32),
            pltpu.VMEM((8, unit, ab_local), jnp.float32),
            pltpu.VMEM((2, 8, far, 16, LANES), jnp.int16),
            pltpu.VMEM((2, 8, far, 16, LANES), jnp.int16),
            pltpu.VMEM((2, 8, near, 16, LANES), jnp.int16),
            pltpu.VMEM((2, 8, near, 16, LANES), jnp.int16),
            dma, dma((cd_local // TCD,)), dma((8,)), dma((10, 2)), dma((STEPS, 2)), dma((STEPS,)), dma((STEPS,)),
            dma((2, 8)), dma((2, 8)), dma((2, 8)), dma((2, 8)),
        ],
        compiler_params=pltpu.CompilerParams(
            collective_id=0, has_side_effects=True, vmem_limit_bytes=60 * 2**20
        ),
    )(ab_sizes, cd_sizes, amplitudes, integrals)
    update = residual / (virt_energy[None, :] - occ_energy[:, None])
    return (residual, update)


def solution(mesh):
    placed = (P("ab", "cd"), P("cd", "ab"), P(), P(), P("ab"), P("cd"))
    return jax.shard_map(
        body, mesh=mesh, in_specs=placed, out_specs=(P("cd", "ab"), P("cd", "ab")), check_vma=False
    )
```

```python
import functools

import jax
import jax.numpy as jnp
from jax import lax
from jax.experimental import pallas as pl
from jax.experimental.pallas import tpu as pltpu
from jax.sharding import PartitionSpec as P

MESH = pl.DeviceIdType.MESH
TCD = 512
LANES = 128
TOP = 32000.0
FINE = 64.0

GROUPS = ((4, 12), (8,)) + tuple((4 * d + 1, 4 * d + 3) for d in range(4)) + tuple((4 * d + 2,) for d in range(4))
PASSED = ((0,), (4, 12), (8,))
STEPS = 16

ACTIONS = (
    (
        5, 4096, 3, 12, 3104, 1, 129, 13, 28, 44, 7328, 33, 11, 2, 320, 130, 21, 36,
        20, 97, 27, 161, 6168, 225, 6056, 65, 34, 193, 43, 7528, 9, 4088, 98, 162, 25, 3600,
        35, 68, 60, 76, 169, 185, 7112, 10, 194, 66, 226, 233, 26, 249, 19, 52, 4392, 17,
        121, 1944, 113, 105, 67, 170, 2512, 59, 137, 41, 201, 217, 18, 5720, 75, 57, 7728, 51,
        73, 202, 4688, 153, 186, 234, 114, 250, 89, 177, 138, 122, 106, 218, 209, 154, 241, 42,
        145, 210, 58, 49, 74, 146, 81, 90, 178, 50, 242, 82,
    ),
    (
        5, 20, 4096, 3, 12, 3104, 1, 13, 44, 7328, 129, 33, 19, 97, 52, 5000, 21, 11,
        2240, 161, 225, 2, 34, 98, 43, 76, 28, 36, 8168, 193, 153, 65, 137, 51, 1832, 75,
        7824, 3944, 130, 66, 162, 154, 226, 233, 145, 249, 138, 27, 60, 6056, 241, 2888, 41, 194,
        57, 105, 146, 121, 35, 68, 6408, 169, 984, 59, 185, 5712, 67, 73, 89, 250, 242, 1744,
        201, 217, 106, 42, 9, 58, 624, 25, 170, 74, 234, 10, 186, 81, 122, 177, 209, 90,
        49, 113, 26, 17, 18, 114, 202, 218, 210, 50, 82, 178,
    ),
)


def pick(table, index):
    words = [low + 8192 * high for low, high in zip(table[::2], table[1::2] + (0,))]
    at = index // 2
    word = words[0]
    for w in range(1, len(words)):
        word = jnp.where(at == w, words[w], word)
    return jnp.where(index % 2 == 0, word, word // 8192) % 8192


def kernel(
    ab_sizes, cd_sizes, amp, integ, out,
    gath, right, acc, nearbuf, resbuf, far_s, far_r, near_s, near_r,
    amp_sem, int_sem, out_sem, ag_s, ag_r, sib_s, sib_r, far_ss, far_rs, near_ss, near_rs,
):
    cd_local, ab_local = right.shape
    unit = amp.shape[0]
    half = unit // 2
    blocks = ab_local // LANES
    index = lax.axis_index("ab")
    y = lax.axis_index("cd")
    c = index % 2
    x = (index // 2) % 4
    z = index // 8

    def at(z_, x_, c_):
        return ((z_ % 4) * 4 + x_ % 4) * 2 + c_

    def along(step):
        return (at(z + step * c, x + step * (1 - c), c), y)

    target = {
        "+": along(1), "-": along(3),
        "core": (at(z, x, 1 - c), y), "y+": (index, (y + 1) % 4), "y-": (index, (y + 3) % 4),
    }

    tile_count = cd_local // TCD

    def int_copy(t):
        rows = pl.ds(pl.multiple_of(t * TCD, TCD), TCD)
        return pltpu.make_async_copy(integ.at[rows], right.at[rows], int_sem.at[t])

    amp_copy = pltpu.make_async_copy(amp, gath.at[0, 0], amp_sem)
    amp_copy.start()
    for t in range(tile_count):
        int_copy(t).start()

    barrier = pltpu.get_barrier_semaphore()
    for name in target:
        pl.semaphore_signal(barrier, inc=1, device_id=target[name], device_id_type=MESH)
    pl.semaphore_wait(barrier, len(target))

    def gather_copy(g, side):
        part = None
        if g == 0:
            source, slot, gather = amp, (12, 4)[side], 0
        elif g == 1:
            source, slot, gather, part = gath.at[(12, 4)[side], 0], 8, 0, side
        elif g < 6:
            d = 4 * (g - 2)
            source, slot, gather = gath.at[d, 1], d + (3, 1)[side], 1
        else:
            d = 4 * (g - 6)
            source, slot, gather, part = gath.at[d + (3, 1)[side], 1], d + 2, 1, side
        dest = gath.at[slot, gather]
        if part is not None:
            source = source.at[pl.ds(part * half, half)]
            dest = dest.at[pl.ds(part * half, half)]
        return pltpu.make_async_remote_copy(
            src_ref=source, dst_ref=dest, send_sem=ag_s.at[g, side], recv_sem=ag_r.at[slot, part or 0],
            device_id=target["-" if side else "+"], device_id_type=MESH,
        )

    def sibling_copy(k):
        gather = 0 if k % 4 == 0 else 1
        return pltpu.make_async_remote_copy(
            src_ref=amp if k == 0 else gath.at[k, gather], dst_ref=gath.at[k, 1 - gather],
            send_sem=sib_s.at[k], recv_sem=sib_r.at[k],
            device_id=target["core"], device_id_type=MESH,
        )

    def issue(g):
        for side in (0, 1):
            gather_copy(g, side).start()

    def handle(g):
        for side in (0, 1):
            gather_copy(g, side).wait_recv()
        for k in GROUPS[g]:
            sibling_copy(k).start()

    def passed(g):
        for k in PASSED[g]:
            pltpu.make_async_remote_copy(
                src_ref=gath.at[k, 1], dst_ref=gath.at[k, 1], send_sem=sib_s.at[k], recv_sem=sib_r.at[k],
                device_id=target["core"], device_id_type=MESH,
            ).wait_recv()

    issue(0)
    sibling_copy(0).start()

    column = index * ab_local + lax.broadcasted_iota(jnp.int32, (1, ab_local), 1)

    def mask_tile(t, carry):
        place = y * cd_local + t * TCD
        low = 0
        high = 0
        end = 0
        for h in range(8):
            size = ab_sizes[h]
            high = high + jnp.where(end <= place, size, 0)
            end = end + cd_sizes[h]
            low = low + jnp.where(end <= place, size, 0)
        keep = jnp.where(jnp.logical_and(column >= low, column < high), 1.0, 0.0).astype(jnp.bfloat16)
        int_copy(t).wait()
        rows = pl.ds(pl.multiple_of(t * TCD, TCD), TCD)
        right[rows, :] = right[rows, :] * keep
        return carry

    lax.fori_loop(0, tile_count, mask_tile, 0)
    amp_copy.wait()

    def unit_place(u):
        net = u // 16
        dp = (u % 16) // 4
        dq = u % 4
        core = (c + net) % 2
        dz = dq + core * (dp - dq)
        dx = dp + core * (dq - dp)
        return (z + dz - y + 8) % 4, ((x + dx) % 4) * 2 + core

    row_of = lax.broadcasted_iota(jnp.int32, (16, LANES), 0)

    def quantize(source, row, rows, dest):
        scales = jnp.zeros((16, LANES), jnp.float32)
        for j in range(blocks):
            value = source[pl.ds(row, rows), pl.ds(j * LANES, LANES)]
            most = jnp.max(jnp.abs(value), axis=0, keepdims=True)
            code = jnp.ceil(jnp.log2(jnp.maximum(most, 1e-30)) * FINE)
            factor = TOP / jnp.exp2(code * (1.0 / FINE))
            whole = jnp.floor(value * factor + 0.5).astype(jnp.int32).astype(jnp.int16)
            for i in range(rows // 16):
                dest[j * (rows // 16) + i] = whole[i * 16 : (i + 1) * 16]
            scales = jnp.where(row_of == j, code, scales)
        dest[blocks * (rows // 16)] = scales.astype(jnp.int32).astype(jnp.int16)

    def scales_of(source, rows):
        code = source[blocks * (rows // 16)].astype(jnp.int32).astype(jnp.float32)
        return jnp.exp2(code * (1.0 / FINE)) * (1.0 / TOP)

    def tiles_of(source, rows, j, scales):
        parts = [source[j * (rows // 16) + i].astype(jnp.int32).astype(jnp.float32) for i in range(rows // 16)]
        return jnp.concatenate(parts, axis=0) * scales[j : j + 1]

    def far_copy(slot, side):
        return pltpu.make_async_remote_copy(
            src_ref=far_s.at[side, slot], dst_ref=far_r.at[side, slot],
            send_sem=far_ss.at[side, slot], recv_sem=far_rs.at[side, slot],
            device_id=target["y-" if side else "y+"], device_id_type=MESH,
        )

    def near_copy(slot, side):
        return pltpu.make_async_remote_copy(
            src_ref=near_s.at[side, slot], dst_ref=near_r.at[side, slot],
            send_sem=near_ss.at[side, slot], recv_sem=near_rs.at[side, slot],
            device_id=target["y-" if side else "y+"], device_id_type=MESH,
        )

    def out_copy(slot):
        rows = pl.ds(pl.multiple_of(slot * unit, unit), unit)
        return pltpu.make_async_copy(resbuf.at[slot], out.at[rows], out_sem.at[slot])

    def after_product(u, net):
        role, slot = unit_place(u)

        @pl.when(role == 2)
        def _():
            for side in (0, 1):
                quantize(acc, net * unit + side * half, half, far_s.at[side, slot])
                far_copy(slot, side).start()

        for side, near in ((0, 1), (1, 3)):

            @pl.when(role == near)
            def _():
                nearbuf[side, slot] = acc[pl.ds(net * unit, unit), :]

        @pl.when(role == 0)
        def _():
            resbuf[slot] = acc[pl.ds(net * unit, unit), :]

    def near_stage(u):
        role, slot = unit_place(u)
        for side, near in ((0, 1), (1, 3)):

            @pl.when(role == near)
            def _():
                far_copy(slot, side).wait_recv()
                arrived = far_r.at[side, slot]
                scales = scales_of(arrived, half)
                for j in range(blocks):
                    cols = pl.ds(j * LANES, LANES)
                    rows = pl.ds(side * half, half)
                    nearbuf[side, slot, rows, cols] = nearbuf[side, slot, rows, cols] + tiles_of(arrived, half, j, scales)
                quantize(nearbuf.at[side, slot], 0, unit, near_s.at[side, slot])
                near_copy(slot, side).start()

    def own_stage(u):
        role, slot = unit_place(u)

        @pl.when(role == 0)
        def _():
            for side in (0, 1):
                near_copy(slot, side).wait_recv()
                arrived = near_r.at[side, slot]
                scales = scales_of(arrived, unit)
                for j in range(blocks):
                    cols = pl.ds(j * LANES, LANES)
                    resbuf[slot, :, cols] = resbuf[slot, :, cols] + tiles_of(arrived, unit, j, scales)
            out_copy(slot).start()

    def product(first, second):
        for u in (first, second):

            @pl.when(jnp.logical_and(u < 16, u % 4 != 0))
            def _():
                pltpu.make_async_remote_copy(
                    src_ref=gath.at[u, 0], dst_ref=gath.at[u, 0], send_sem=sib_s.at[u], recv_sem=sib_r.at[u],
                    device_id=target["core"], device_id_type=MESH,
                ).wait_recv()

        left = jnp.concatenate([gath[u % 16, u // 16] for u in (first, second)], axis=0)
        acc[...] = jnp.dot(left, right[...], preferred_element_type=jnp.float32)
        after_product(first, 0)
        after_product(second, 1)

    def act(a, carry):
        code = jnp.where(c == 0, pick(ACTIONS[0], a), pick(ACTIONS[1], a))
        kind = code % 8
        arg = (code // 8) % 32

        @pl.when(kind == 0)
        def _():
            product(arg, code // 256)

        @pl.when(kind == 1)
        def _():
            near_stage(arg)

        @pl.when(kind == 2)
        def _():
            own_stage(arg)

        for this, count, do in ((3, len(GROUPS), handle), (4, len(GROUPS), issue), (5, len(PASSED), passed)):

            @pl.when(kind == this)
            def _():
                for g in range(count):

                    @pl.when(arg == g)
                    def _():
                        do(g)

        return carry

    lax.fori_loop(0, len(ACTIONS[0]), act, 0)

    for g in range(len(GROUPS)):
        for side in (0, 1):
            gather_copy(g, side).wait_send()
    for k in range(STEPS):
        sibling_copy(k).wait_send()

    def finish(slot, carry):
        for side in (0, 1):
            far_copy(slot, side).wait_send()
            near_copy(slot, side).wait_send()
        out_copy(slot).wait()
        return carry

    lax.fori_loop(0, 8, finish, 0)


def divide(sums, virt, occ, residual, update):
    rows = jnp.concatenate([jnp.transpose(jnp.broadcast_to(occ[pl.ds(pl.multiple_of(pl.program_id(0) * 256 + i * LANES, LANES), LANES)].reshape(1, LANES), (LANES, LANES))) for i in range(256 // LANES)], axis=0)
    for j in range(sums.shape[1] // LANES):
        cols = pl.ds(j * LANES, LANES)
        value = sums[:, cols]
        residual[:, cols] = value
        update[:, cols] = value / (virt[cols].reshape(1, LANES) - rows)


def body(amplitudes, integrals, ab_sizes, cd_sizes, virt_energy, occ_energy):
    cd_local, ab_local = integrals.shape
    unit = amplitudes.shape[0]
    rows = occ_energy.shape[0]
    blocks = ab_local // LANES
    far = blocks * (unit // 32) + 1
    near = blocks * (unit // 16) + 1
    dma = pltpu.SemaphoreType.DMA
    residual = pl.pallas_call(
        kernel,
        out_shape=jax.ShapeDtypeStruct((rows, ab_local), jnp.float32),
        in_specs=[pl.BlockSpec(memory_space=pltpu.SMEM)] * 2 + [pl.BlockSpec(memory_space=pl.ANY)] * 2,
        out_specs=pl.BlockSpec(memory_space=pl.ANY),
        scratch_shapes=[
            pltpu.VMEM((STEPS, 2, unit, cd_local), jnp.bfloat16),
            pltpu.VMEM((cd_local, ab_local), jnp.bfloat16),
            pltpu.VMEM((2 * unit, ab_local), jnp.float32),
            pltpu.VMEM((2, 8, unit, ab_local), jnp.float32),
            pltpu.VMEM((8, unit, ab_local), jnp.float32),
            pltpu.VMEM((2, 8, far, 16, LANES), jnp.int16),
            pltpu.VMEM((2, 8, far, 16, LANES), jnp.int16),
            pltpu.VMEM((2, 8, near, 16, LANES), jnp.int16),
            pltpu.VMEM((2, 8, near, 16, LANES), jnp.int16),
            dma, dma((cd_local // TCD,)), dma((8,)), dma((10, 2)), dma((STEPS, 2)), dma((STEPS,)), dma((STEPS,)),
            dma((2, 8)), dma((2, 8)), dma((2, 8)), dma((2, 8)),
        ],
        compiler_params=pltpu.CompilerParams(
            collective_id=0, has_side_effects=True, vmem_limit_bytes=60 * 2**20
        ),
    )(ab_sizes, cd_sizes, amplitudes, integrals)
    tile = pl.BlockSpec((256, ab_local), lambda i: (i, 0))
    return pl.pallas_call(
        divide,
        grid=(rows // 256,),
        out_shape=(jax.ShapeDtypeStruct((rows, ab_local), jnp.float32),) * 2,
        in_specs=[tile, pl.BlockSpec((ab_local,), lambda i: (0,)), pl.BlockSpec((rows,), lambda i: (0,))],
        out_specs=(tile, tile),
        compiler_params=pltpu.CompilerParams(vmem_limit_bytes=60 * 2**20),
    )(residual, virt_energy, occ_energy)


def solution(mesh):
    placed = (P("ab", "cd"), P("cd", "ab"), P(), P(), P("ab"), P("cd"))
    return jax.shard_map(
        body, mesh=mesh, in_specs=placed, out_specs=(P("cd", "ab"), P("cd", "ab")), check_vma=False
    )
```

```python
import functools

import jax
import jax.numpy as jnp
from jax import lax
from jax.experimental import pallas as pl
from jax.experimental.pallas import tpu as pltpu
from jax.sharding import PartitionSpec as P

MESH = pl.DeviceIdType.MESH
TCD = 512
LANES = 128
TOP = 32000.0
FINE = 64.0

COPIES = (
    ("first", 0, 0), ("first", 0, 1), ("across", 0, None), ("second", 0, None), ("second", 1, 0), ("second", 1, 1),
    ("second", 2, None), ("second", 3, 0), ("second", 3, 1), ("last", 0, None), ("last", 1, None), ("last", 2, None),
    ("last", 3, None),
)
ARRIVALS = (
    ((0,), (4, 12), 0), ((1,), (4, 12), 1), ((2,), (8,), None), ((3,), (1, 3), None), ((4, 5), (5, 7), None),
    ((6,), (9, 11), None), ((7, 8), (13, 15), None), ((9,), (2,), None), ((10,), (6,), None), ((11,), (10,), None),
    ((12,), (14,), None),
)
PASSED = (((0,), None), ((4, 12), 0), ((4, 12), 1), ((8,), None))
STEPS = 16

UNITS = (
    (
        0, 16, 4, 12, 20, 28, 8, 1, 3, 24, 21, 23, 13, 29, 31, 15, 2, 14, 25, 27, 5, 17, 19, 7, 26, 9,
        11, 22, 6, 30, 10, 18,
    ),
    (
        0, 16, 4, 12, 20, 28, 17, 19, 24, 8, 29, 31, 5, 7, 18, 30, 13, 15, 21, 23, 9, 11, 1, 25, 27, 3,
        10, 22, 26, 6, 14, 2,
    ),
)
ACTIONS = (
    (
        5, 0, 3, 11, 20, 8, 1, 9, 13, 21, 36, 44, 60, 68, 16, 17, 19, 2, 24, 10, 29, 52, 28, 25, 35, 33,
        32, 41, 40, 49, 18, 73, 51, 48, 57, 56, 26, 34, 65, 64, 43, 92, 84, 100, 81, 89, 72, 58, 74, 50, 42, 105,
        66, 113, 27, 76, 80, 129, 121, 88, 137, 97, 75, 82, 96, 67, 169, 161, 145, 153, 130, 104, 83, 185, 112, 59, 201, 146,
        120, 177, 90, 106, 138, 114, 209, 217, 170, 122, 98, 154, 193, 178, 233, 162, 249, 194, 186, 225, 202, 250, 241, 210, 218, 226,
        234, 242,
    ),
    (
        5, 28, 0, 3, 11, 20, 8, 1, 13, 21, 60, 68, 16, 9, 17, 27, 25, 76, 24, 29, 19, 32, 33, 41, 2, 18,
        26, 51, 100, 36, 44, 52, 40, 65, 57, 73, 49, 59, 48, 83, 56, 64, 10, 74, 34, 58, 42, 81, 113, 89, 50, 35,
        84, 72, 121, 80, 97, 66, 105, 129, 114, 137, 43, 92, 88, 145, 96, 67, 153, 104, 75, 161, 169, 90, 122, 112, 185, 193,
        130, 98, 177, 106, 120, 201, 146, 162, 82, 178, 154, 209, 138, 217, 225, 170, 233, 241, 202, 249, 250, 242, 186, 194, 226, 234,
        210, 218,
    ),
)
PLACE = tuple({u: i for i, u in enumerate(units)} for units in UNITS)


def pick(table, bits, index):
    words = []
    for w in range(0, len(table), 4):
        word = sum(v << (bits * i) for i, v in enumerate(table[w : w + 4]))
        words.append(word - 2**32 if word >= 2**31 else word)
    at = index >> 2
    word = words[0]
    for w in range(1, len(words)):
        word = jnp.where(at == w, words[w], word)
    return (word >> ((index & 3) * bits)) & (2**bits - 1)


def kernel(
    ab_sizes, cd_sizes, amp, integ, out,
    gath, right, acc, nearbuf, resbuf, far_s, far_r, near_s, near_r,
    amp_sem, int_sem, out_sem, ag_s, ag_r, sib_s, sib_r, far_ss, far_rs, near_ss, near_rs,
):
    cd_local, ab_local = right.shape
    unit = amp.shape[0]
    half = unit // 2
    blocks = ab_local // LANES
    index = lax.axis_index("ab")
    y = lax.axis_index("cd")
    c = index % 2
    x = (index // 2) % 4
    z = index // 8

    def at(z_, x_, c_):
        return ((z_ % 4) * 4 + x_ % 4) * 2 + c_

    def along(step):
        return (at(z + step * c, x + step * (1 - c), c), y)

    target = {
        "+": along(1), "-": along(3),
        "core": (at(z, x, 1 - c), y), "y+": (index, (y + 1) % 4), "y-": (index, (y + 3) % 4),
    }

    tile_count = cd_local // TCD

    def int_copy(t):
        rows = pl.ds(pl.multiple_of(t * TCD, TCD), TCD)
        return pltpu.make_async_copy(integ.at[rows], right.at[rows], int_sem.at[t])

    amp_copy = pltpu.make_async_copy(amp, gath.at[jnp.where(c == 0, PLACE[0][0], PLACE[1][0])], amp_sem)
    amp_copy.start()
    for t in range(tile_count):
        int_copy(t).start()

    barrier = pltpu.get_barrier_semaphore()
    for name in target:
        pl.semaphore_signal(barrier, inc=1, device_id=target[name], device_id_type=MESH)
    pl.semaphore_wait(barrier, len(target))

    def place(k, gather, core=0):
        unit_at = k + 16 * (gather if core == 0 else 1 - gather)
        return gath.at[jnp.where(c == core, PLACE[0][unit_at], PLACE[1][unit_at])]

    def rows_of(ref, part):
        return ref if part is None else ref.at[pl.ds(part * half, half)]

    def gather_copy(g, side):
        what, d, part = COPIES[g]
        if what == "first":
            source, slot, gather = amp, (12, 4)[side], 0
        elif what == "across":
            source, slot, gather, part = place((12, 4)[side], 0), 8, 0, side
        elif what == "second":
            source, slot, gather = place(4 * d, 1), 4 * d + (3, 1)[side], 1
        else:
            source, slot, gather, part = place(4 * d + (3, 1)[side], 1), 4 * d + 2, 1, side
        return pltpu.make_async_remote_copy(
            src_ref=rows_of(source, part), dst_ref=rows_of(place(slot, gather), part),
            send_sem=ag_s.at[g, side], recv_sem=ag_r.at[slot, part or 0],
            device_id=target["-" if side else "+"], device_id_type=MESH,
        )

    def sibling_copy(k, part):
        gather = 0 if k % 4 == 0 else 1
        return pltpu.make_async_remote_copy(
            src_ref=rows_of(amp if k == 0 else place(k, gather), part), dst_ref=rows_of(place(k, gather, 1), part),
            send_sem=sib_s.at[k, part or 0], recv_sem=sib_r.at[k, part or 0],
            device_id=target["core"], device_id_type=MESH,
        )

    def issue(g):
        for side in (0, 1):
            gather_copy(g, side).start()

    def handle(g):
        groups, slots, part = ARRIVALS[g]
        for group in groups:
            for side in (0, 1):
                gather_copy(group, side).wait_recv()
        for k in slots:
            sibling_copy(k, part).start()

    def passed(g):
        slots, part = PASSED[g]
        for k in slots:
            sibling_copy(k, part).wait_recv()

    issue(0)
    issue(1)
    sibling_copy(0, None).start()

    column = index * ab_local + lax.broadcasted_iota(jnp.int32, (1, ab_local), 1)

    def mask_tile(t, carry):
        place = y * cd_local + t * TCD
        low = 0
        high = 0
        end = 0
        for h in range(8):
            size = ab_sizes[h]
            high = high + jnp.where(end <= place, size, 0)
            end = end + cd_sizes[h]
            low = low + jnp.where(end <= place, size, 0)
        keep = jnp.where(jnp.logical_and(column >= low, column < high), 1.0, 0.0).astype(jnp.bfloat16)
        int_copy(t).wait()
        rows = pl.ds(pl.multiple_of(t * TCD, TCD), TCD)
        right[rows, :] = right[rows, :] * keep
        return carry

    lax.fori_loop(0, tile_count, mask_tile, 0)
    amp_copy.wait()

    def unit_of(i):
        return jnp.where(c == 0, pick(UNITS[0], 5, i), pick(UNITS[1], 5, i))

    def unit_place(i):
        u = unit_of(i)
        net = u // 16
        dp = (u % 16) // 4
        dq = u % 4
        core = (c + net) % 2
        dz = dq + core * (dp - dq)
        dx = dp + core * (dq - dp)
        return (z + dz - y + 8) % 4, ((x + dx) % 4) * 2 + core

    row_of = lax.broadcasted_iota(jnp.int32, (16, LANES), 0)

    def quantize(source, row, rows, dest):
        scales = jnp.zeros((16, LANES), jnp.float32)
        for j in range(blocks):
            value = source[pl.ds(row, rows), pl.ds(j * LANES, LANES)]
            most = jnp.max(jnp.abs(value), axis=0, keepdims=True)
            code = jnp.ceil(jnp.log2(jnp.maximum(most, 1e-30)) * FINE)
            factor = TOP / jnp.exp2(code * (1.0 / FINE))
            whole = jnp.floor(value * factor + 0.5).astype(jnp.int32).astype(jnp.int16)
            for i in range(rows // 16):
                dest[j * (rows // 16) + i] = whole[i * 16 : (i + 1) * 16]
            scales = jnp.where(row_of == j, code, scales)
        dest[blocks * (rows // 16)] = scales.astype(jnp.int32).astype(jnp.int16)

    def scales_of(source, rows):
        code = source[blocks * (rows // 16)].astype(jnp.int32).astype(jnp.float32)
        return jnp.exp2(code * (1.0 / FINE)) * (1.0 / TOP)

    def tiles_of(source, rows, j, scales):
        parts = [source[j * (rows // 16) + i].astype(jnp.int32).astype(jnp.float32) for i in range(rows // 16)]
        return jnp.concatenate(parts, axis=0) * scales[j : j + 1]

    def far_copy(slot, side):
        return pltpu.make_async_remote_copy(
            src_ref=far_s.at[side, slot], dst_ref=far_r.at[side, slot],
            send_sem=far_ss.at[side, slot], recv_sem=far_rs.at[side, slot],
            device_id=target["y-" if side else "y+"], device_id_type=MESH,
        )

    def near_copy(slot, side):
        return pltpu.make_async_remote_copy(
            src_ref=near_s.at[side, slot], dst_ref=near_r.at[side, slot],
            send_sem=near_ss.at[side, slot], recv_sem=near_rs.at[side, slot],
            device_id=target["y-" if side else "y+"], device_id_type=MESH,
        )

    def out_copy(slot):
        rows = pl.ds(pl.multiple_of(slot * unit, unit), unit)
        return pltpu.make_async_copy(resbuf.at[slot], out.at[rows], out_sem.at[slot])

    def after_product(u, net):
        role, slot = unit_place(u)

        @pl.when(role == 2)
        def _():
            for side in (0, 1):
                quantize(acc, net * unit + side * half, half, far_s.at[side, slot])
                far_copy(slot, side).start()

        for side, near in ((0, 1), (1, 3)):

            @pl.when(role == near)
            def _():
                nearbuf[side, slot] = acc[pl.ds(net * unit, unit), :]

        @pl.when(role == 0)
        def _():
            resbuf[slot] = acc[pl.ds(net * unit, unit), :]

    def near_stage(u):
        role, slot = unit_place(u)
        for side, near in ((0, 1), (1, 3)):

            @pl.when(role == near)
            def _():
                far_copy(slot, side).wait_recv()
                arrived = far_r.at[side, slot]
                scales = scales_of(arrived, half)
                for j in range(blocks):
                    cols = pl.ds(j * LANES, LANES)
                    rows = pl.ds(side * half, half)
                    nearbuf[side, slot, rows, cols] = nearbuf[side, slot, rows, cols] + tiles_of(arrived, half, j, scales)
                quantize(nearbuf.at[side, slot], 0, unit, near_s.at[side, slot])
                near_copy(slot, side).start()

    def own_stage(u):
        role, slot = unit_place(u)

        @pl.when(role == 0)
        def _():
            for side in (0, 1):
                near_copy(slot, side).wait_recv()
                arrived = near_r.at[side, slot]
                scales = scales_of(arrived, unit)
                for j in range(blocks):
                    cols = pl.ds(j * LANES, LANES)
                    resbuf[slot, :, cols] = resbuf[slot, :, cols] + tiles_of(arrived, unit, j, scales)
            out_copy(slot).start()

    def product(p):
        for i in (2 * p, 2 * p + 1):
            u = unit_of(i)

            @pl.when(jnp.logical_and(u < 16, u % 4 != 0))
            def _():
                pltpu.make_async_remote_copy(
                    src_ref=gath.at[i], dst_ref=gath.at[i], send_sem=sib_s.at[u, 0], recv_sem=sib_r.at[u, 0],
                    device_id=target["core"], device_id_type=MESH,
                ).wait_recv()

        left = gath[pl.ds(2 * p, 2)].reshape(2 * unit, cd_local)
        acc[...] = jnp.dot(left, right[...], preferred_element_type=jnp.float32)
        after_product(2 * p, 0)
        after_product(2 * p + 1, 1)

    def act(a, carry):
        code = jnp.where(c == 0, pick(ACTIONS[0], 8, a), pick(ACTIONS[1], 8, a))
        kind = code & 7
        arg = code >> 3

        @pl.when(kind == 0)
        def _():
            product(arg)

        @pl.when(kind == 1)
        def _():
            near_stage(arg)

        @pl.when(kind == 2)
        def _():
            own_stage(arg)

        for this, count, do in ((3, len(ARRIVALS), handle), (4, len(COPIES), issue), (5, len(PASSED), passed)):

            @pl.when(kind == this)
            def _():
                for g in range(count):

                    @pl.when(arg == g)
                    def _():
                        do(g)

        return carry

    lax.fori_loop(0, len(ACTIONS[0]), act, 0)

    for g in range(len(COPIES)):
        for side in (0, 1):
            gather_copy(g, side).wait_send()
    for k in range(STEPS):
        for part in (0, 1) if k in (4, 12) else (None,):
            sibling_copy(k, part).wait_send()

    def finish(slot, carry):
        for side in (0, 1):
            far_copy(slot, side).wait_send()
            near_copy(slot, side).wait_send()
        out_copy(slot).wait()
        return carry

    lax.fori_loop(0, 8, finish, 0)


def divide(sums, virt, occ, residual, update):
    rows = jnp.concatenate([jnp.transpose(jnp.broadcast_to(occ[pl.ds(pl.multiple_of(pl.program_id(0) * 256 + i * LANES, LANES), LANES)].reshape(1, LANES), (LANES, LANES))) for i in range(256 // LANES)], axis=0)
    for j in range(sums.shape[1] // LANES):
        cols = pl.ds(j * LANES, LANES)
        value = sums[:, cols]
        residual[:, cols] = value
        update[:, cols] = value / (virt[cols].reshape(1, LANES) - rows)


def body(amplitudes, integrals, ab_sizes, cd_sizes, virt_energy, occ_energy):
    cd_local, ab_local = integrals.shape
    unit = amplitudes.shape[0]
    rows = occ_energy.shape[0]
    blocks = ab_local // LANES
    far = blocks * (unit // 32) + 1
    near = blocks * (unit // 16) + 1
    dma = pltpu.SemaphoreType.DMA
    residual = pl.pallas_call(
        kernel,
        out_shape=jax.ShapeDtypeStruct((rows, ab_local), jnp.float32),
        in_specs=[pl.BlockSpec(memory_space=pltpu.SMEM)] * 2 + [pl.BlockSpec(memory_space=pl.ANY)] * 2,
        out_specs=pl.BlockSpec(memory_space=pl.ANY),
        scratch_shapes=[
            pltpu.VMEM((2 * STEPS, unit, cd_local), jnp.bfloat16),
            pltpu.VMEM((cd_local, ab_local), jnp.bfloat16),
            pltpu.VMEM((2 * unit, ab_local), jnp.float32),
            pltpu.VMEM((2, 8, unit, ab_local), jnp.float32),
            pltpu.VMEM((8, unit, ab_local), jnp.float32),
            pltpu.VMEM((2, 8, far, 16, LANES), jnp.int16),
            pltpu.VMEM((2, 8, far, 16, LANES), jnp.int16),
            pltpu.VMEM((2, 8, near, 16, LANES), jnp.int16),
            pltpu.VMEM((2, 8, near, 16, LANES), jnp.int16),
            dma, dma((cd_local // TCD,)), dma((8,)), dma((len(COPIES), 2)), dma((STEPS, 2)), dma((STEPS, 2)), dma((STEPS, 2)),
            dma((2, 8)), dma((2, 8)), dma((2, 8)), dma((2, 8)),
        ],
        compiler_params=pltpu.CompilerParams(
            collective_id=0, has_side_effects=True, vmem_limit_bytes=60 * 2**20
        ),
    )(ab_sizes, cd_sizes, amplitudes, integrals)
    tile = pl.BlockSpec((256, ab_local), lambda i: (i, 0))
    return pl.pallas_call(
        divide,
        grid=(rows // 256,),
        out_shape=(jax.ShapeDtypeStruct((rows, ab_local), jnp.float32),) * 2,
        in_specs=[tile, pl.BlockSpec((ab_local,), lambda i: (0,)), pl.BlockSpec((rows,), lambda i: (0,))],
        out_specs=(tile, tile),
        compiler_params=pltpu.CompilerParams(vmem_limit_bytes=60 * 2**20),
    )(residual, virt_energy, occ_energy)


def solution(mesh):
    placed = (P("ab", "cd"), P("cd", "ab"), P(), P(), P("ab"), P("cd"))
    return jax.shard_map(
        body, mesh=mesh, in_specs=placed, out_specs=(P("cd", "ab"), P("cd", "ab")), check_vma=False
    )
```

```python
import functools

import jax
import jax.numpy as jnp
from jax import lax
from jax.experimental import pallas as pl
from jax.experimental.pallas import tpu as pltpu
from jax.sharding import PartitionSpec as P

MESH = pl.DeviceIdType.MESH
TCD = 512
LANES = 128
TOP = 32000.0
FINE = 64.0

COPIES = (
    ("first", 0, 0), ("first", 0, 1), ("across", 0, None), ("second", 0, None), ("second", 1, 0), ("second", 1, 1),
    ("second", 2, None), ("second", 3, 0), ("second", 3, 1), ("last", 0, None), ("last", 1, None), ("last", 2, None),
    ("last", 3, None),
)
ARRIVALS = (
    ((0,), (4, 12), 0), ((1,), (4, 12), 1), ((2,), (8,), None), ((3,), (1, 3), None), ((4, 5), (5, 7), None),
    ((6,), (9, 11), None), ((7, 8), (13, 15), None), ((9,), (2,), None), ((10,), (6,), None), ((11,), (10,), None),
    ((12,), (14,), None),
)
PASSED = (((0,), None), ((4, 12), 0), ((4, 12), 1), ((8,), None))
STEPS = 16

UNITS = (
    (
        0, 16, 4, 12, 20, 28, 8, 24, 29, 31, 13, 15, 25, 27, 5, 7, 14, 21, 23, 6, 17, 19, 1, 26, 3, 22,
        9, 18, 11, 30, 2, 10,
    ),
    (
        0, 16, 4, 12, 20, 28, 8, 24, 29, 31, 13, 15, 21, 23, 9, 30, 11, 22, 5, 7, 17, 19, 1, 3, 10, 25,
        27, 6, 18, 2, 26, 14,
    ),
)
ACTIONS = (
    (
        5, 0, 3, 11, 20, 8, 1, 9, 13, 21, 60, 68, 16, 17, 19, 25, 2, 29, 52, 36, 44, 28, 24, 10, 33, 51,
        32, 41, 18, 57, 49, 40, 34, 26, 43, 92, 48, 42, 56, 65, 58, 97, 35, 84, 64, 73, 105, 72, 81, 113, 89, 50,
        27, 76, 100, 80, 137, 98, 121, 66, 106, 75, 88, 129, 145, 67, 96, 153, 161, 169, 74, 82, 59, 104, 114, 90, 138, 83,
        112, 177, 193, 130, 122, 146, 162, 120, 201, 185, 225, 233, 217, 170, 154, 209, 194, 178, 241, 186, 249, 218, 202, 226, 242, 234,
        210, 250,
    ),
    (
        5, 0, 3, 11, 20, 8, 1, 13, 21, 60, 68, 36, 44, 16, 9, 17, 19, 25, 29, 24, 33, 41, 2, 18, 26, 51,
        100, 32, 49, 57, 40, 10, 35, 84, 28, 52, 48, 34, 83, 56, 65, 73, 42, 50, 67, 64, 58, 113, 97, 72, 121, 27,
        76, 80, 81, 89, 105, 129, 66, 137, 88, 74, 145, 114, 43, 92, 96, 169, 98, 104, 59, 122, 153, 161, 82, 130, 112, 75,
        138, 90, 120, 177, 185, 209, 146, 106, 201, 193, 154, 170, 162, 249, 217, 225, 233, 178, 241, 186, 226, 210, 194, 202, 234, 242,
        218, 250,
    ),
)
PLACE = tuple({u: i for i, u in enumerate(units)} for units in UNITS)


def pick(table, bits, index):
    words = []
    for w in range(0, len(table), 4):
        word = sum(v << (bits * i) for i, v in enumerate(table[w : w + 4]))
        words.append(word - 2**32 if word >= 2**31 else word)
    at = index >> 2
    word = words[0]
    for w in range(1, len(words)):
        word = jnp.where(at == w, words[w], word)
    return (word >> ((index & 3) * bits)) & (2**bits - 1)


def kernel(
    ab_sizes, cd_sizes, amp, integ, out,
    gath, right, acc, nearbuf, resbuf, far_s, far_r, near_s, near_r,
    amp_sem, int_sem, out_sem, ag_s, ag_r, sib_s, sib_r, far_ss, far_rs, near_ss, near_rs,
):
    cd_local, ab_local = right.shape
    unit = amp.shape[0]
    half = unit // 2
    blocks = ab_local // LANES
    index = lax.axis_index("ab")
    y = lax.axis_index("cd")
    c = index % 2
    x = (index // 2) % 4
    z = index // 8

    def at(z_, x_, c_):
        return ((z_ % 4) * 4 + x_ % 4) * 2 + c_

    def along(step):
        return (at(z + step * c, x + step * (1 - c), c), y)

    target = {
        "+": along(1), "-": along(3),
        "core": (at(z, x, 1 - c), y), "y+": (index, (y + 1) % 4), "y-": (index, (y + 3) % 4),
    }

    tile_count = cd_local // TCD

    def int_copy(t):
        rows = pl.ds(pl.multiple_of(t * TCD, TCD), TCD)
        return pltpu.make_async_copy(integ.at[rows], right.at[rows], int_sem.at[t])

    amp_copy = pltpu.make_async_copy(amp, gath.at[jnp.where(c == 0, PLACE[0][0], PLACE[1][0])], amp_sem)
    amp_copy.start()
    for t in range(tile_count):
        int_copy(t).start()

    barrier = pltpu.get_barrier_semaphore()
    for name in target:
        pl.semaphore_signal(barrier, inc=1, device_id=target[name], device_id_type=MESH)
    pl.semaphore_wait(barrier, len(target))

    def place(k, gather, core=0):
        unit_at = k + 16 * (gather if core == 0 else 1 - gather)
        return gath.at[jnp.where(c == core, PLACE[0][unit_at], PLACE[1][unit_at])]

    def rows_of(ref, part):
        return ref if part is None else ref.at[pl.ds(part * half, half)]

    def gather_copy(g, side):
        what, d, part = COPIES[g]
        if what == "first":
            source, slot, gather = amp, (12, 4)[side], 0
        elif what == "across":
            source, slot, gather, part = place((12, 4)[side], 0), 8, 0, side
        elif what == "second":
            source, slot, gather = place(4 * d, 1), 4 * d + (3, 1)[side], 1
        else:
            source, slot, gather, part = place(4 * d + (3, 1)[side], 1), 4 * d + 2, 1, side
        return pltpu.make_async_remote_copy(
            src_ref=rows_of(source, part), dst_ref=rows_of(place(slot, gather), part),
            send_sem=ag_s.at[g, side], recv_sem=ag_r.at[slot, part or 0],
            device_id=target["-" if side else "+"], device_id_type=MESH,
        )

    def sibling_copy(k, part):
        gather = 0 if k % 4 == 0 else 1
        return pltpu.make_async_remote_copy(
            src_ref=rows_of(amp if k == 0 else place(k, gather), part), dst_ref=rows_of(place(k, gather, 1), part),
            send_sem=sib_s.at[k, part or 0], recv_sem=sib_r.at[k, part or 0],
            device_id=target["core"], device_id_type=MESH,
        )

    def issue(g):
        for side in (0, 1):
            gather_copy(g, side).start()

    def handle(g):
        groups, slots, part = ARRIVALS[g]
        for group in groups:
            for side in (0, 1):
                gather_copy(group, side).wait_recv()
        for k in slots:
            sibling_copy(k, part).start()

    def passed(g):
        slots, part = PASSED[g]
        for k in slots:
            sibling_copy(k, part).wait_recv()

    issue(0)
    issue(1)
    sibling_copy(0, None).start()

    column = index * ab_local + lax.broadcasted_iota(jnp.int32, (1, ab_local), 1)

    def mask_tile(t, carry):
        place = y * cd_local + t * TCD
        low = 0
        high = 0
        end = 0
        for h in range(8):
            size = ab_sizes[h]
            high = high + jnp.where(end <= place, size, 0)
            end = end + cd_sizes[h]
            low = low + jnp.where(end <= place, size, 0)
        keep = jnp.where(jnp.logical_and(column >= low, column < high), 1.0, 0.0).astype(jnp.bfloat16)
        int_copy(t).wait()
        rows = pl.ds(pl.multiple_of(t * TCD, TCD), TCD)
        right[rows, :] = right[rows, :] * keep
        return carry

    lax.fori_loop(0, tile_count, mask_tile, 0)
    amp_copy.wait()

    def unit_of(i):
        return jnp.where(c == 0, pick(UNITS[0], 5, i), pick(UNITS[1], 5, i))

    def unit_place(i):
        u = unit_of(i)
        net = u // 16
        dp = (u % 16) // 4
        dq = u % 4
        core = (c + net) % 2
        dz = dq + core * (dp - dq)
        dx = dp + core * (dq - dp)
        return (z + dz - y + 8) % 4, ((x + dx) % 4) * 2 + core

    row_of = lax.broadcasted_iota(jnp.int32, (16, LANES), 0)

    def quantize(source, row, rows, dest):
        scales = jnp.zeros((16, LANES), jnp.float32)
        for j in range(blocks):
            value = source[pl.ds(row, rows), pl.ds(j * LANES, LANES)]
            most = jnp.max(jnp.abs(value), axis=0, keepdims=True)
            code = jnp.ceil(jnp.log2(jnp.maximum(most, 1e-30)) * FINE)
            factor = TOP / jnp.exp2(code * (1.0 / FINE))
            whole = jnp.floor(value * factor + 0.5).astype(jnp.int32).astype(jnp.int16)
            for i in range(rows // 16):
                dest[j * (rows // 16) + i] = whole[i * 16 : (i + 1) * 16]
            scales = jnp.where(row_of == j, code, scales)
        dest[blocks * (rows // 16)] = scales.astype(jnp.int32).astype(jnp.int16)

    def scales_of(source, rows):
        code = source[blocks * (rows // 16)].astype(jnp.int32).astype(jnp.float32)
        return jnp.exp2(code * (1.0 / FINE)) * (1.0 / TOP)

    def tiles_of(source, rows, j, scales):
        parts = [source[j * (rows // 16) + i].astype(jnp.int32).astype(jnp.float32) for i in range(rows // 16)]
        return jnp.concatenate(parts, axis=0) * scales[j : j + 1]

    def far_copy(slot, side):
        return pltpu.make_async_remote_copy(
            src_ref=far_s.at[side, slot], dst_ref=far_r.at[side, slot],
            send_sem=far_ss.at[side, slot], recv_sem=far_rs.at[side, slot],
            device_id=target["y-" if side else "y+"], device_id_type=MESH,
        )

    def near_copy(slot, side):
        return pltpu.make_async_remote_copy(
            src_ref=near_s.at[side, slot], dst_ref=near_r.at[side, slot],
            send_sem=near_ss.at[side, slot], recv_sem=near_rs.at[side, slot],
            device_id=target["y-" if side else "y+"], device_id_type=MESH,
        )

    def out_copy(slot):
        rows = pl.ds(pl.multiple_of(slot * unit, unit), unit)
        return pltpu.make_async_copy(resbuf.at[slot], out.at[rows], out_sem.at[slot])

    def after_product(u, net):
        role, slot = unit_place(u)

        @pl.when(role == 2)
        def _():
            for side in (0, 1):
                quantize(acc, net * unit + side * half, half, far_s.at[side, slot])
                far_copy(slot, side).start()

        for side, near in ((0, 1), (1, 3)):

            @pl.when(role == near)
            def _():
                nearbuf[side, slot] = acc[pl.ds(net * unit, unit), :]

        @pl.when(role == 0)
        def _():
            resbuf[slot] = acc[pl.ds(net * unit, unit), :]

    def near_stage(u):
        role, slot = unit_place(u)
        for side, near in ((0, 1), (1, 3)):

            @pl.when(role == near)
            def _():
                far_copy(slot, side).wait_recv()
                arrived = far_r.at[side, slot]
                scales = scales_of(arrived, half)
                for j in range(blocks):
                    cols = pl.ds(j * LANES, LANES)
                    rows = pl.ds(side * half, half)
                    nearbuf[side, slot, rows, cols] = nearbuf[side, slot, rows, cols] + tiles_of(arrived, half, j, scales)
                quantize(nearbuf.at[side, slot], 0, unit, near_s.at[side, slot])
                near_copy(slot, side).start()

    def own_stage(u):
        role, slot = unit_place(u)

        @pl.when(role == 0)
        def _():
            for side in (0, 1):
                near_copy(slot, side).wait_recv()
                arrived = near_r.at[side, slot]
                scales = scales_of(arrived, unit)
                for j in range(blocks):
                    cols = pl.ds(j * LANES, LANES)
                    resbuf[slot, :, cols] = resbuf[slot, :, cols] + tiles_of(arrived, unit, j, scales)
            out_copy(slot).start()

    def product(p):
        for i in (2 * p, 2 * p + 1):
            u = unit_of(i)

            @pl.when(jnp.logical_and(u < 16, u % 4 != 0))
            def _():
                pltpu.make_async_remote_copy(
                    src_ref=gath.at[i], dst_ref=gath.at[i], send_sem=sib_s.at[u, 0], recv_sem=sib_r.at[u, 0],
                    device_id=target["core"], device_id_type=MESH,
                ).wait_recv()

        left = gath[pl.ds(2 * p, 2)].reshape(2 * unit, cd_local)
        acc[...] = jnp.dot(left, right[...], preferred_element_type=jnp.float32)
        after_product(2 * p, 0)
        after_product(2 * p + 1, 1)

    def act(a, carry):
        code = jnp.where(c == 0, pick(ACTIONS[0], 8, a), pick(ACTIONS[1], 8, a))
        kind = code & 7
        arg = code >> 3

        @pl.when(kind == 0)
        def _():
            product(arg)

        @pl.when(kind == 1)
        def _():
            near_stage(arg)

        @pl.when(kind == 2)
        def _():
            own_stage(arg)

        for this, count, do in ((3, len(ARRIVALS), handle), (4, len(COPIES), issue), (5, len(PASSED), passed)):

            @pl.when(kind == this)
            def _():
                for g in range(count):

                    @pl.when(arg == g)
                    def _():
                        do(g)

        return carry

    lax.fori_loop(0, len(ACTIONS[0]), act, 0)

    for g in range(len(COPIES)):
        for side in (0, 1):
            gather_copy(g, side).wait_send()
    for k in range(STEPS):
        for part in (0, 1) if k in (4, 12) else (None,):
            sibling_copy(k, part).wait_send()

    def finish(slot, carry):
        for side in (0, 1):
            far_copy(slot, side).wait_send()
            near_copy(slot, side).wait_send()
        out_copy(slot).wait()
        return carry

    lax.fori_loop(0, 8, finish, 0)


def divide(sums, virt, occ, residual, update):
    rows = jnp.concatenate([jnp.transpose(jnp.broadcast_to(occ[pl.ds(pl.multiple_of(pl.program_id(0) * 256 + i * LANES, LANES), LANES)].reshape(1, LANES), (LANES, LANES))) for i in range(256 // LANES)], axis=0)
    for j in range(sums.shape[1] // LANES):
        cols = pl.ds(j * LANES, LANES)
        value = sums[:, cols]
        residual[:, cols] = value
        update[:, cols] = value / (virt[cols].reshape(1, LANES) - rows)


def body(amplitudes, integrals, ab_sizes, cd_sizes, virt_energy, occ_energy):
    cd_local, ab_local = integrals.shape
    unit = amplitudes.shape[0]
    rows = occ_energy.shape[0]
    blocks = ab_local // LANES
    far = blocks * (unit // 32) + 1
    near = blocks * (unit // 16) + 1
    dma = pltpu.SemaphoreType.DMA
    residual = pl.pallas_call(
        kernel,
        out_shape=jax.ShapeDtypeStruct((rows, ab_local), jnp.float32),
        in_specs=[pl.BlockSpec(memory_space=pltpu.SMEM)] * 2 + [pl.BlockSpec(memory_space=pl.ANY)] * 2,
        out_specs=pl.BlockSpec(memory_space=pl.ANY),
        scratch_shapes=[
            pltpu.VMEM((2 * STEPS, unit, cd_local), jnp.bfloat16),
            pltpu.VMEM((cd_local, ab_local), jnp.bfloat16),
            pltpu.VMEM((2 * unit, ab_local), jnp.float32),
            pltpu.VMEM((2, 8, unit, ab_local), jnp.float32),
            pltpu.VMEM((8, unit, ab_local), jnp.float32),
            pltpu.VMEM((2, 8, far, 16, LANES), jnp.int16),
            pltpu.VMEM((2, 8, far, 16, LANES), jnp.int16),
            pltpu.VMEM((2, 8, near, 16, LANES), jnp.int16),
            pltpu.VMEM((2, 8, near, 16, LANES), jnp.int16),
            dma, dma((cd_local // TCD,)), dma((8,)), dma((len(COPIES), 2)), dma((STEPS, 2)), dma((STEPS, 2)), dma((STEPS, 2)),
            dma((2, 8)), dma((2, 8)), dma((2, 8)), dma((2, 8)),
        ],
        compiler_params=pltpu.CompilerParams(
            collective_id=0, has_side_effects=True, vmem_limit_bytes=60 * 2**20
        ),
    )(ab_sizes, cd_sizes, amplitudes, integrals)
    tile = pl.BlockSpec((256, ab_local), lambda i: (i, 0))
    return pl.pallas_call(
        divide,
        grid=(rows // 256,),
        out_shape=(jax.ShapeDtypeStruct((rows, ab_local), jnp.float32),) * 2,
        in_specs=[tile, pl.BlockSpec((ab_local,), lambda i: (0,)), pl.BlockSpec((rows,), lambda i: (0,))],
        out_specs=(tile, tile),
        compiler_params=pltpu.CompilerParams(vmem_limit_bytes=60 * 2**20),
    )(residual, virt_energy, occ_energy)


def solution(mesh):
    placed = (P("ab", "cd"), P("cd", "ab"), P(), P(), P("ab"), P("cd"))
    return jax.shard_map(
        body, mesh=mesh, in_specs=placed, out_specs=(P("cd", "ab"), P("cd", "ab")), check_vma=False
    )
```
